32 devices in a mesh: dp: 16 (over z, y, core), dir: 2 (over x).
Axes of the slice: x: 2, y: 2, z: 4, core: 2. Of those that a mesh axis runs over, the one named last changes fastest.
Arguments:
- tokens: bfloat16 [8192, 768], P(('dp', 'dir')), may hold values from -6 to 6
- layernorm_gain: float32 [768], replicated, may hold values from 0.5 to 1.5
- layernorm_bias: float32 [768], replicated, may hold values from -3 to 3
- up_weight: bfloat16 [768, 3072], replicated, may hold values from -0.21875 to 0.21875
- up_bias: float32 [3072], replicated, may hold values from -3 to 3
- value_weight: bfloat16 [768, 1536], replicated, may hold values from -0.21875 to 0.21875
- value_bias: float32 [1536], replicated, may hold values from -3 to 3
- step_log: float32 [1536], replicated, may hold values from -4.6 to -2.3
- decay_log: float32 [1536, 64], replicated, may hold values from -1 to 1
- frequency: float32 [1536, 64], replicated, may hold values from 0 to 50
- coef_real: float32 [1536, 64], replicated, may hold values from -3 to 3
- coef_imag: float32 [1536, 64], replicated, may hold values from -3 to 3
- skip_gain: float32 [1536], replicated, may hold values from -4 to 4
- gate_weight: bfloat16 [3072, 1536], replicated, may hold values from -0.109375 to 0.109375
- gate_bias: float32 [1536], replicated, may hold values from -3 to 3
- out_weight: bfloat16 [1536, 768], replicated, may hold values from -0.15625 to 0.15625
- out_bias: float32 [768], replicated, may hold values from -3 to 3
- cotangent: bfloat16 [8192, 768], P(('dp', 'dir')), may hold values from -6 to 6
Outputs:
- mixed: bfloat16 [8192, 768], P(('dp', 'dir'))
- grad_tokens: bfloat16 [8192, 768], P(('dp', 'dir'))
- grad_norm_gain: float32 [768], replicated
- grad_norm_bias: float32 [768], replicated
- grad_up_weight: float32 [768, 3072], P(('dp', 'dir'))
- grad_up_bias: float32 [3072], P(('dp', 'dir'))
- grad_value_weight: float32 [768, 1536], P(('dp', 'dir'))
- grad_value_bias: float32 [1536], P(('dp', 'dir'))
- grad_step_log: float32 [1536], P(('dp', 'dir'))
- grad_decay_log: float32 [1536, 64], P(('dp', 'dir'))
- grad_frequency: float32 [1536, 64], P(('dp', 'dir'))
- grad_coef_real: float32 [1536, 64], P(('dp', 'dir'))
- grad_coef_imag: float32 [1536, 64], P(('dp', 'dir'))
- grad_skip_gain: float32 [1536], P(('dp', 'dir'))
- grad_gate_weight: float32 [3072, 1536], P(('dp', 'dir'))
- grad_gate_bias: float32 [1536], P(('dp', 'dir'))
- grad_out_weight: float32 [1536, 768], P(('dp', 'dir'))
- grad_out_bias: float32 [768], replicated
The draws below stay inside these ranges and needn't reach their ends.
All inputs are finite; a program needn't handle non-finite values.
Results may differ from the reference program's by a relative error of at most 0.0082.
Values may be sent and summed in bfloat16 or wider, within the bound.
No kernel may reach another device: no remote copies, remote signals or barrier semaphores. Data moves between devices by JAX's collectives and lax.ppermute only.
A program may use at most 256 MiB of HBM per device.

```python
import math
import jax
import jax.numpy as jnp
from jax import lax

D = 768
HID = 3072
CH = 1536
STATE = 64
SEQ_LEN = 128
TOKENS = 8192


def strengthened(result, rng, source, target, parts, factor):
    owner, partner = [(jnp.arange(result.shape[position]) // (result.shape[position] // parts)).reshape([-1 if axis == position else 1 for axis in range(result.ndim)]) for position in (source, target)]
    chosen = jax.random.permutation(rng, parts)[partner]
    strong = (owner == chosen) | (owner == (partner + parts // 2) % parts)
    return jnp.where(strong, factor * result, result)


def levels(own_key, extent, shards, least, high):
    gain = 1.0
    for position, shards_of in shards:
        heights = jax.random.uniform(jax.random.fold_in(jax.random.fold_in(own_key, 6), position), (shards_of,), jnp.float32, least / len(shards), high / len(shards))
        gain = gain * jnp.repeat(jnp.exp(heights), extent[position] // shards_of).reshape((-1,) + (1,) * (len(extent) - 1 - position))
    return gain


def noise(own_key, dims, scale, reach, cuts=(), kind=jnp.bfloat16):
    level = levels(own_key, dims, cuts, -0.22, 0.18) if cuts else 1.0
    values = jax.random.normal(own_key, dims, jnp.float32) * scale * level
    return jnp.minimum(jnp.maximum(values, -reach), reach).astype(kind)


def gaussian_with(own_key, dims, deviation, most, cuts, heavy, dtype=jnp.bfloat16):
    drawn = deviation * jax.random.normal(own_key, dims, jnp.float32)
    if cuts:
        drawn = drawn * levels(own_key, dims, cuts, -0.22, 0.18)
    return jnp.clip(strengthened(drawn, jax.random.fold_in(own_key, 3), *heavy), -most, most).astype(dtype)


def setup_inputs(seed: int = 0) -> dict:
    splits = jax.random.split(jax.random.key(seed), 19)
    return {
        "tokens": noise(splits[0], (TOKENS, D), 1.0, 6.0, ((0, 32),)),
        "layernorm_gain": jnp.clip(1.0 + 0.1 * jax.random.normal(splits[1], (D,), jnp.float32), 0.5, 1.5),
        "layernorm_bias": noise(splits[2], (D,), 0.5, 3.0, (), jnp.float32),
        "up_weight": noise(splits[3], (D, HID), D ** -0.5, 0.21875),
        "up_bias": noise(splits[4], (HID,), 0.5, 3.0, (), jnp.float32),
        "value_weight": noise(splits[5], (D, CH), D ** -0.5, 0.21875),
        "value_bias": noise(splits[6], (CH,), 0.5, 3.0, (), jnp.float32),
        "step_log": jnp.clip(jax.random.uniform(splits[7], (CH,), jnp.float32, -4.6, -2.3), -4.6, -2.3),
        "decay_log": jnp.clip(jax.random.uniform(splits[8], (CH, STATE), jnp.float32, -1.0, 1.0), -1.0, 1.0),
        "frequency": jnp.clip(jax.random.uniform(splits[9], (CH, STATE), jnp.float32, 0.0, 50.0), 0.0, 50.0),
        "coef_real": noise(splits[10], (CH, STATE), 0.5, 3.0, (), jnp.float32),
        "coef_imag": noise(splits[11], (CH, STATE), 0.5, 3.0, (), jnp.float32),
        "skip_gain": noise(splits[12], (CH,), 1.0, 4.0, (), jnp.float32),
        "gate_weight": noise(splits[13], (HID, CH), HID ** -0.5, 0.109375),
        "gate_bias": noise(splits[14], (CH,), 0.5, 3.0, (), jnp.float32),
        "out_weight": noise(splits[15], (CH, D), CH ** -0.5, 0.15625),
        "out_bias": noise(splits[16], (D,), 0.5, 3.0, (), jnp.float32),
        "cotangent": gaussian_with(splits[17], (TOKENS, D), 1.0, 6.0, ((0, 32),), (0, 1, 32, 2.75)),
    }


eps = 1e-05

@jax.custom_vjp
def low(v):
    return lax.optimization_barrier(v.astype(jnp.bfloat16)).astype(jnp.float32)

@jax.custom_vjp
def low_back(v):
    return v

def low_keep(v):
    return (low(v), None)

def low_pass(kept, grad):
    return (grad,)

def back_keep(v):
    return (v, None)

def back_low(kept, grad):
    return (low(grad),)
low.defvjp(low_keep, low_pass)
low_back.defvjp(back_keep, back_low)

def kernel_rows(step_log, decay_log, frequency, coef_real, coef_imag, length):
    delta = jnp.exp(step_log)[:, None, None]
    lags = jnp.arange(length).astype(jnp.float32)[None, None, :]
    rate = jnp.exp(decay_log)[:, :, None]
    phase = frequency[:, :, None] * delta * lags
    damp = jnp.exp(-rate * delta * lags)
    terms = damp * (coef_real[:, :, None] * jnp.cos(phase) - coef_imag[:, :, None] * jnp.sin(phase))
    return delta[:, :, 0] * lax.optimization_barrier(jnp.sum(terms, axis=1))

def toeplitz(kern, flip):
    length = kern.shape[1]
    rows_idx = jnp.arange(length).astype(jnp.int32)[:, None]
    cols_idx = jnp.arange(length).astype(jnp.int32)[None, :]
    gap = rows_idx - cols_idx
    table = jnp.take(kern, jnp.clip(gap, 0, length - 1), axis=1)
    table = jnp.where(gap[None] >= 0, table, jnp.zeros_like(table))
    return jnp.where(flip, jnp.swapaxes(table, 1, 2), table)

def layer(inputs, layernorm_gain, layernorm_bias, up_weight, up_bias, value_weight, value_bias, step_log, decay_log, frequency, coef_real, coef_imag, skip_gain, gate_weight, gate_bias, out_weight, out_bias):
    highest = lax.Precision.HIGHEST
    feature_average = lax.optimization_barrier(jnp.mean(inputs, axis=1, keepdims=True))
    centered_input = inputs - feature_average
    inverse_deviation = lax.rsqrt(lax.optimization_barrier(jnp.mean(centered_input * centered_input, axis=1, keepdims=True)) + eps)
    normalized_input = low(centered_input * inverse_deviation * layernorm_gain + layernorm_bias)
    up_pre = low_back(jnp.dot(normalized_input, up_weight, precision=highest) + up_bias)
    up_act = low(jax.nn.gelu(up_pre, approximate=False))
    value_pre = low_back(jnp.dot(normalized_input, value_weight, precision=highest) + value_bias)
    value_act = low_back(low(jax.nn.gelu(value_pre, approximate=False)))
    kern = low(kernel_rows(step_log, decay_log, frequency, coef_real, coef_imag, SEQ_LEN))
    chans = kern.shape[0]
    flip = (jnp.arange(chans) >= chans // 2)[:, None, None]
    table = toeplitz(kern, flip)
    value_seq = value_act.reshape(-1, SEQ_LEN, chans)
    mixed_seq = jnp.einsum('cts,nsc->ntc', table, value_seq, precision=highest) + skip_gain * value_seq
    ssm_out = low_back(low(mixed_seq.reshape(inputs.shape[0], chans)))
    gate_pre = low_back(jnp.dot(up_act, gate_weight, precision=highest) + gate_bias)
    gated = low(gate_pre * ssm_out)
    return inputs + jnp.dot(gated, out_weight, precision=highest) + out_bias

def reference(tokens, layernorm_gain, layernorm_bias, up_weight, up_bias, value_weight, value_bias, step_log, decay_log, frequency, coef_real, coef_imag, skip_gain, gate_weight, gate_bias, out_weight, out_bias, cotangent):
    weights = (layernorm_gain, layernorm_bias, up_weight.astype(jnp.float32), up_bias, value_weight.astype(jnp.float32), value_bias, step_log, decay_log, frequency, coef_real, coef_imag, skip_gain, gate_weight.astype(jnp.float32), gate_bias, out_weight.astype(jnp.float32), out_bias)
    per = math.gcd(TOKENS // SEQ_LEN, 32) * SEQ_LEN
    blocks = TOKENS // per
    inputs = tokens.astype(jnp.float32).reshape(blocks, per, D)
    cots = cotangent.astype(jnp.float32).reshape(blocks, per, D)

    def step(total, pair):
        block_in, block_cot = pair
        out, back = jax.vjp(layer, block_in, *weights)
        grads = back(block_cot)
        summed = tuple((a + b for a, b in zip(total, grads[1:])))
        return (summed, (out.astype(jnp.bfloat16), grads[0].astype(jnp.bfloat16)))
    start = tuple((jnp.zeros_like(w) for w in weights))
    total, (outs, grad_in) = lax.scan(step, start, (inputs, cots))
    mixed = outs.reshape(TOKENS, D)
    grad_tokens = grad_in.reshape(TOKENS, D)
    return (mixed, grad_tokens, total[0], total[1], total[2], total[3], total[4], total[5], total[6], total[7], total[8], total[9], total[10], total[11], total[12], total[13], total[14], total[15])
```

```python
import math

import jax
import jax.numpy as jnp
import numpy as np
from jax import lax
from jax.sharding import PartitionSpec as P

SEQ_LEN = 128
AXES = ("dp", "dir")

eps = 1e-05
root_half = 0.7071067811865476
inv_root_two_pi = 0.3989422804014327
bf16 = jnp.bfloat16
f32 = jnp.float32


def gelu_slope(v):
    return 0.5 * (1.0 + lax.erf(v * root_half)) + v * inv_root_two_pi * jnp.exp(-0.5 * v * v)


def kernel_rows(step_log, decay_log, frequency, coef_real, coef_imag, length):
    delta = jnp.exp(step_log)[:, None, None]
    lags = jnp.arange(length).astype(f32)[None, None, :]
    rate = jnp.exp(decay_log)[:, :, None]
    phase = frequency[:, :, None] * delta * lags
    damp = jnp.exp(-rate * delta * lags)
    terms = damp * (coef_real[:, :, None] * jnp.cos(phase) - coef_imag[:, :, None] * jnp.sin(phase))
    return delta[:, :, 0] * jnp.sum(terms, axis=1)


def fourier(length):
    freq = np.arange(length)[:, None] + 0.5
    time = np.arange(length)[None, :]
    angle = np.pi * freq * time / length
    ahead = np.concatenate([np.cos(angle), -np.sin(angle)], axis=0)
    back = np.concatenate([np.cos(angle), -np.sin(angle)], axis=0).T / length
    return ahead.astype(np.float32), back.astype(np.float32)


def local(
    n_dp,
    n_dir,
    tokens,
    layernorm_gain,
    layernorm_bias,
    up_weight,
    up_bias,
    value_weight,
    value_bias,
    step_log,
    decay_log,
    frequency,
    coef_real,
    coef_imag,
    skip_gain,
    gate_weight,
    gate_bias,
    out_weight,
    out_bias,
    cotangent,
):
    rows, width = tokens.shape
    chans = value_weight.shape[1]
    hidden = up_weight.shape[1]
    length = SEQ_LEN
    seqs = rows // length
    n = n_dp * n_dir
    nbits = int(math.log2(n))
    me = lax.axis_index("dp") * n_dir + lax.axis_index("dir")
    bit = [(me >> b) & 1 for b in range(nbits)]
    X, C, Y = 0, 1, 2
    rest = list(range(3, nbits))
    highest = lax.Precision.HIGH

    def swap(a, b):
        return lax.ppermute(a, AXES, [(j, j ^ (1 << b)) for j in range(n)])

    def part(a, which):
        half = a.shape[0] // 2
        return lax.dynamic_slice_in_dim(a, which * half, half, 0)

    def ordered(a, order):
        a = a.reshape((2,) * nbits + (a.shape[0] // n,) + a.shape[1:])
        axes = [nbits - 1 - b for b in order] + list(range(nbits, a.ndim))
        a = a.transpose(axes)
        return a.reshape((-1,) + a.shape[nbits + 1 :])

    def reduce_rest(keep, recv, order):
        for b in order:
            send = part(keep, 1 - bit[b]) + part(recv, 1 - bit[b])
            keep, recv = part(keep, bit[b]) + part(recv, bit[b]), swap(send, b)
        return keep.astype(f32) + recv.astype(f32)

    def grad_scatter(lhs, rhs, order):
        lhs_in = swap(part(lhs, 1 - bit[C]), C)
        lhs_own = part(lhs, bit[C])
        rhs_in = swap(rhs, C)
        lhs2 = jnp.concatenate([lhs_own, lhs_in], axis=1)
        rhs2 = jnp.concatenate([rhs, rhs_in], axis=0)
        b = order[1]
        send = jnp.dot(part(lhs2, 1 - bit[b]), rhs2, preferred_element_type=f32).astype(bf16)
        recv = swap(send, b)
        keep = jnp.dot(part(lhs2, bit[b]), rhs2, preferred_element_type=f32).astype(bf16)
        return reduce_rest(keep, recv, order[2:])

    own = chans // n
    mine = [
        lax.dynamic_slice_in_dim(p, me * own, own, 0)
        for p in (step_log, decay_log, frequency, coef_real, coef_imag)
    ]
    kern_own, kern_back = jax.vjp(lambda p: kernel_rows(*p, length), tuple(mine))
    kern = kern_own.astype(bf16).reshape((1,) * nbits + (own, length))
    for b in rest[::-1] + [Y, X, C]:
        other = swap(kern, b)
        axis = nbits - 1 - b
        kern = jnp.where(
            bit[b] == 1,
            jnp.concatenate([other, kern], axis=axis),
            jnp.concatenate([kern, other], axis=axis),
        )
    kern = kern.reshape(chans, length)

    ahead, back = fourier(length)
    ahead_all = jnp.asarray(np.kron(np.eye(seqs), ahead).astype(np.float32))
    back_all = jnp.asarray(np.kron(np.eye(seqs), back).astype(np.float32))
    ahead, back = jnp.asarray(ahead), jnp.asarray(back)
    turn = jnp.where(jnp.arange(chans) < chans // 2, 1.0, -1.0).astype(f32)

    def spectrum(a):
        s = jnp.dot(ahead_all, a.astype(f32), precision=highest).reshape(seqs, 2, length, chans)
        return s[:, 0], s[:, 1]

    def unspectrum(re, im):
        s = jnp.stack([re, im], axis=1).reshape(seqs * 2 * length, chans)
        return jnp.dot(back_all, s, precision=highest)

    kern_hat = lax.dot_general(
        ahead, kern.astype(f32), (((1,), (1,)), ((), ())), precision=highest
    ).reshape(2, length, chans)
    kr, ki = kern_hat[0], kern_hat[1] * turn

    inputs = tokens.astype(f32)
    average = jnp.mean(inputs, axis=1, keepdims=True)
    centered = inputs - average
    deviation = lax.rsqrt(jnp.mean(centered * centered, axis=1, keepdims=True) + eps)
    xhat = centered * deviation
    normed = (xhat * layernorm_gain + layernorm_bias).astype(bf16)
    up_pre = jnp.dot(normed, up_weight, preferred_element_type=f32) + up_bias
    up_act = jax.nn.gelu(up_pre, approximate=False).astype(bf16)
    value_pre = jnp.dot(normed, value_weight, preferred_element_type=f32) + value_bias
    value_act = jax.nn.gelu(value_pre, approximate=False).astype(bf16)
    gate_pre = jnp.dot(up_act, gate_weight, preferred_element_type=f32) + gate_bias
    d_gated = lax.dot_general(
        cotangent, out_weight, (((1,), (1,)), ((), ())), preferred_element_type=f32
    )
    vr, vi = spectrum(value_act)
    ssm_out = (
        unspectrum(kr * vr - ki * vi, kr * vi + ki * vr) + skip_gain * value_act.astype(f32)
    ).astype(bf16)
    ssm_wide = ssm_out.astype(f32)
    gated = (gate_pre * ssm_wide).astype(bf16)
    d_gate = (d_gated * ssm_wide).astype(bf16)
    d_ssm = (d_gated * gate_pre).astype(bf16)

    gate_order = [C, X, Y] + rest
    gate_share = grad_scatter(ordered(up_act.T, gate_order), d_gate, gate_order)
    out_order = [C] + rest + [X, Y]
    out_share = grad_scatter(ordered(gated.T, out_order), cotangent, out_order)

    dr, di = spectrum(d_ssm)
    d_value = (
        unspectrum(kr * dr + ki * di, kr * di - ki * dr) + skip_gain * d_ssm.astype(f32)
    )
    gr = jnp.sum(dr * vr + di * vi, axis=0)
    gi = jnp.sum(di * vr - dr * vi, axis=0) * turn
    grad_kern = lax.dot_general(
        jnp.concatenate([gr, gi], axis=0), back, (((0,), (1,)), ((), ())), precision=highest
    )
    kern_order = [C, X, Y] + rest
    grad_kern = ordered(grad_kern, kern_order)
    b = kern_order[0]
    grad_kern = reduce_rest(part(grad_kern, bit[b]), swap(part(grad_kern, 1 - bit[b]), b), kern_order[1:])

    d_up = lax.dot_general(
        d_gate, gate_weight, (((1,), (1,)), ((), ())), preferred_element_type=f32
    )
    d_up_pre = (d_up * gelu_slope(up_pre)).astype(bf16)
    d_value_pre = (d_value.astype(bf16).astype(f32) * gelu_slope(value_pre)).astype(bf16)
    both = jnp.concatenate([d_up_pre, d_value_pre], axis=1)
    input_order = [C, Y, X] + rest
    input_share = grad_scatter(ordered(normed.T, input_order), both, input_order)

    d_normed = lax.dot_general(
        d_up_pre, up_weight, (((1,), (1,)), ((), ())), preferred_element_type=f32
    ) + lax.dot_general(
        d_value_pre, value_weight, (((1,), (1,)), ((), ())), preferred_element_type=f32
    )
    scaled = d_normed * layernorm_gain
    inner = (
        scaled
        - jnp.mean(scaled, axis=1, keepdims=True)
        - xhat * jnp.mean(scaled * xhat, axis=1, keepdims=True)
    )
    grad_tokens = (cotangent.astype(f32) + deviation * inner).astype(bf16)
    mixed = (
        inputs + jnp.dot(gated, out_weight, preferred_element_type=f32) + out_bias
    ).astype(bf16)

    vectors = [
        jnp.sum(d_normed * xhat, axis=0),
        jnp.sum(d_normed, axis=0),
        jnp.sum(cotangent.astype(f32), axis=0),
        jnp.sum(d_up_pre.astype(f32), axis=0),
        jnp.sum(d_value_pre.astype(f32), axis=0),
        jnp.sum(d_gate.astype(f32), axis=0),
        jnp.sum(d_ssm.astype(f32) * value_act.astype(f32), axis=0),
    ]
    packed = jnp.concatenate(vectors).reshape(-1, 128)
    for b in range(nbits):
        packed = packed + swap(packed, b)
    packed = packed.reshape(-1)
    sums, at = [], 0
    for v in vectors:
        sums.append(packed[at : at + v.shape[0]])
        at += v.shape[0]

    def share(v):
        size = v.shape[0] // n
        return lax.dynamic_slice_in_dim(v, me * size, size, 0)

    steps, decays, frequencies, reals, imags = kern_back(grad_kern)[0]
    return (
        mixed,
        grad_tokens,
        sums[0],
        sums[1],
        input_share[:, :hidden],
        share(sums[3]),
        input_share[:, hidden:],
        share(sums[4]),
        steps,
        decays,
        frequencies,
        reals,
        imags,
        share(sums[6]),
        gate_share,
        share(sums[5]),
        out_share,
        sums[2],
    )


def solution(mesh):
    n_dp, n_dir = mesh.shape["dp"], mesh.shape["dir"]
    split, whole = P(AXES), P()
    in_specs = (split,) + (whole,) * 16 + (split,)
    out_specs = (split, split, whole, whole) + (split,) * 13 + (whole,)

    def run(*args):
        return local(n_dp, n_dir, *args)

    return jax.shard_map(run, mesh=mesh, in_specs=in_specs, out_specs=out_specs, check_vma=False)
```

```python
import functools
import math

import jax
import jax.numpy as jnp
import numpy as np
from jax import lax
from jax.experimental import pallas as pl
from jax.experimental.pallas import tpu as pltpu
from jax.sharding import PartitionSpec as P

SEQ_LEN = 128
AXES = ("dp", "dir")
LANES = 128
MIB = 1 << 20

eps = 1e-05
root_half = 0.7071067811865476
inv_root_two_pi = 0.3989422804014327
bf16 = jnp.bfloat16
f32 = jnp.float32


def fourier(length):
    freq = np.arange(length)[:, None] + 0.5
    time = np.arange(length)[None, :]
    angle = np.pi * freq * time / length
    ahead = np.concatenate([np.cos(angle), -np.sin(angle)], axis=0)
    return ahead, ahead.T / length


def in_two(a):
    high = a.astype(np.float32).astype(jnp.bfloat16)
    low = (a - high.astype(np.float64)).astype(np.float32).astype(jnp.bfloat16)
    return high, low


def mm(a, b):
    return jnp.dot(a, b, preferred_element_type=f32)


def mm_t(a, b):
    return lax.dot_general(a, b, (((1,), (1,)), ((), ())), preferred_element_type=f32)


def spec(shape, index):
    return pl.BlockSpec(shape, index)


def in_hbm(*arrays):
    return [pltpu.with_memory_space_constraint(a, pltpu.HBM) for a in arrays]


def whole(shape):
    return pl.BlockSpec(shape, lambda *_: (0,) * len(shape))


def params(mib=56):
    return pltpu.CompilerParams(vmem_limit_bytes=mib * MIB)


def row(ref, first=0, count=None):
    count = ref.shape[0] if count is None else count
    return ref[pl.ds(first, count)].reshape(1, count)


BLOCK = 768


def took(us):
    return pl.CostEstimate(flops=int(us * 1e9), bytes_accessed=int(us * 3e6), transcendentals=0)


def sort_place(block, me, order):
    apart = block ^ me
    place = 0
    for b in order:
        place = place * 2 + ((apart >> b) & 1)
    return place


def sort_block(place, me, order):
    block = 0
    for k, b in enumerate(order):
        block = block | (((place >> (len(order) - 1 - k)) & 1) << b)
    return block ^ me


def rows_kernel(me, step, *rest):
    sources, (out, held, zs, sems) = rest[:4], rest[4:]
    i = pl.program_id(0)
    blocks = pl.num_programs(0)
    span = held.shape[-1]
    quarter = pl.multiple_of((me[0] & 3) * span, LANES)
    copies = [pltpu.make_async_copy(s.at[:, pl.ds(quarter, span)], held.at[k], sems.at[k]) for k, s in enumerate(sources)]

    @pl.when(i == 0)
    def _():
        for c in copies:
            c.start()
        for c in copies:
            c.wait()

    here = pl.multiple_of(i * LANES, LANES)
    decay, freq, real, imag = [held[k, :, pl.ds(here, LANES)] for k in range(4)]
    delta = jnp.exp(row(step, pl.multiple_of(quarter + here, LANES), LANES))
    rate = jnp.exp(decay)
    damp = jnp.exp(-rate * delta)
    angle = freq * delta
    zr, zi = damp * jnp.cos(angle), damp * jnp.sin(angle)
    for k in range(4):
        zs[2 * k], zs[2 * k + 1] = zr, zi
        zr, zi = zr * zr - zi * zi, 2.0 * zr * zi
    zs[8], zs[9] = real, imag
    zs[10], zs[11] = 2.0 * zs[6], zs[6] * zs[6] + zs[7] * zs[7]
    states = zs.shape[1]
    sub = lax.broadcasted_iota(jnp.int32, (8, LANES), 0)
    picks = [(sub >> k) % 2 == 1 for k in range(3)]
    count = SEQ_LEN // 8
    group = 4

    def body(step_no, accs):
        accs = list(accs)
        ys = []
        for u in range(group):
            n = step_no * group + u
            row = lambda k: jnp.broadcast_to(zs[k, pl.ds(n, 1), :], (8, LANES))
            wr, wi = row(8), row(9)
            for k in range(3):
                pr = jnp.where(picks[k], row(2 * k), 1.0)
                pi = jnp.where(picks[k], row(2 * k + 1), 0.0)
                wr, wi = wr * pr - wi * pi, wr * pi + wi * pr
            ys.append((wr, wr * row(6) - wi * row(7), row(10), row(11)))
        for a in range(count):
            accs[a] = accs[a] + ((ys[0][0] + ys[1][0]) + (ys[2][0] + ys[3][0]))
            if a < count - 1:
                ys = [(after, p * after - q * now, p, q) for now, after, p, q in ys]
        return tuple(accs)

    accs = lax.fori_loop(0, states // group, body, tuple(jnp.zeros((8, LANES), f32) for _ in range(count)))
    out[0] = (jnp.concatenate(accs, axis=0) * delta).astype(bf16)


def kernel_rows(me, step, decay_t, freq_t, real_t, imag_t):
    states, chans = decay_t.shape
    blocks = chans // 4 // LANES
    return pl.pallas_call(
        rows_kernel,
        grid_spec=pltpu.PrefetchScalarGridSpec(
            num_scalar_prefetch=1,
            grid=(blocks,),
            in_specs=[whole(step.shape)] + [pl.BlockSpec(memory_space=pltpu.HBM)] * 4,
            out_specs=spec((1, SEQ_LEN, LANES), lambda i, m: (i, 0, 0)),
            scratch_shapes=[
                pltpu.VMEM((4, states, chans // 4), f32),
                pltpu.VMEM((12, states, LANES), f32),
                pltpu.SemaphoreType.DMA((4,)),
            ],
        ),
        out_shape=jax.ShapeDtypeStruct((blocks, SEQ_LEN, LANES), bf16),
        compiler_params=params(8),
        cost_estimate=took(4),
        name="kernel_rows",
    )(me, step, *in_hbm(decay_t, freq_t, real_t, imag_t))


def gelu_both(v):
    size = jnp.abs(v)
    bell = jnp.exp(-0.5 * v * v)
    t = 1.0 / (1.0 + (0.3275911 * root_half) * size)
    poly = t * (0.127414796 + t * (-0.142248368 + t * (0.7107068705 + t * (-0.7265760135 + t * 0.5307027145))))
    tail = poly * bell
    phi = jnp.where(v >= 0.0, 1.0 - tail, tail)
    return v * phi, phi + (inv_root_two_pi * v) * bell


def norm_of(inputs):
    centered = inputs - jnp.mean(inputs, axis=1, keepdims=True)
    deviation = lax.rsqrt(jnp.mean(centered * centered, axis=1, keepdims=True) + eps)
    return centered * deviation, deviation


def scatter_blocks(source, me, order, first, own, send):
    size, half = own.shape[1], own.shape[0]
    for b in range(source.shape[0] // size):
        place = sort_place(first + b, me, order)
        block = source[b * size : (b + 1) * size]

        @pl.when(place < half)
        def _():
            own[place] = block

        @pl.when(place >= half)
        def _():
            send[place - half] = block


def project_kernel(
    counts, order, aligned, me, tokens, gain, bias, row_place, row_rest, up_b, val_b, gate_b, cot, up_hbm, val_hbm, out_hbm, gate_hbm,
    up_slope, val_act, val_slope, d_gated, gate_pre, low_own, low_send, *rest,
):
    *turned, normed, act, up_w, val_w, out_w, gate_w, sems = rest
    n_up, n_val, n_out, n_gate = counts
    block = BLOCK
    j = pl.program_id(0)
    per = gate_w.shape[0] // n_up

    copies = []
    for k in range(n_up):
        copies.append((up_hbm.at[:, pl.ds(k * block, block)], up_w.at[k]))
    for k in range(n_val):
        copies.append((val_hbm.at[:, pl.ds(k * block, block)], val_w.at[k]))
    for k in range(n_out):
        copies.append((out_hbm.at[pl.ds(k * block, block)], out_w.at[k]))
    for k in range(n_up):
        copies.append((gate_hbm.at[pl.ds(k * per, per)], gate_w.at[pl.ds(k * per, per)]))
    copies = [pltpu.make_async_copy(a, b, sems.at[i]) for i, (a, b) in enumerate(copies)]

    @pl.when(j == 0)
    def _():
        for c in copies:
            c.start()
        xhat, _ = norm_of(tokens[...].astype(f32))
        normed[...] = (xhat * row(gain) + row(bias)).astype(bf16)
        width = tokens.shape[1]
        lanes = sort_block(row_place[...], me[0], order) * per_block(width, order) + row_rest[...]
        pick = jnp.where(lax.broadcasted_iota(jnp.int32, (width, width), 0) == lanes, 1.0, 0.0).astype(bf16)
        sorted_rows = mm(normed[...], pick).T.astype(bf16)
        low_own[...] = sorted_rows[: width // 2]
        low_send[...] = sorted_rows[width // 2 :]

    for k in range(n_up):

        @pl.when(j == k)
        def _():
            copies[k].wait()

    @pl.when(j < n_up)
    def _():
        out, slope = gelu_both(mm(normed[...], up_w[j]) + row(up_b, pl.multiple_of(j * block, block), block))
        act[j] = out.astype(bf16)
        up_slope[...] = slope.astype(up_slope.dtype)
        flipped = out.T.astype(bf16)
        if aligned:
            own, send = turned
            scatter_blocks(flipped, me[0], order, j * (flipped.shape[0] // own.shape[1]), own, send)
        else:
            turned[0][...] = flipped

    at = n_up
    for k in range(n_val):

        @pl.when(j == at + k)
        def _():
            copies[n_up + k].wait()
            out, slope = gelu_both(mm(normed[...], val_w[k]) + row(val_b, k * block, block))
            val_act[...] = out.astype(bf16)
            val_slope[...] = slope.astype(val_slope.dtype)

    at += n_val
    for k in range(n_out):

        @pl.when(j == at + k)
        def _():
            copies[n_up + n_val + k].wait()
            d_gated[...] = mm_t(cot[...], out_w[k])

    at += n_out
    for k in range(n_gate):

        @pl.when(j == at + k)
        def _():
            if k == 0:
                for c in copies[n_up + n_val + n_out :]:
                    c.wait()
            columns = slice(k * block, (k + 1) * block)
            total = row(gate_b, k * block, block) + mm(act[0], gate_w[:per, columns])
            for i in range(1, n_up):
                total = total + mm(act[i], gate_w[i * per : (i + 1) * per, columns])
            gate_pre[...] = total


def per_block(width, order):
    return width >> len(order)


def project(me, order, vectors, tokens, cot, up_weight, value_weight, out_weight, gate_weight):
    rows, width = tokens.shape
    hidden, chans = gate_weight.shape
    n = 1 << len(order)
    block = BLOCK
    n_up, n_val = hidden // block, chans // block
    counts = (n_up, n_val, n_val, n_val)
    size = hidden // n
    aligned = size % 16 == 0
    clip = lambda j, first, count: jnp.clip(j - first, 0, count - 1)
    up_at = lambda j, m: (0, clip(j, 0, n_up))
    val_at = lambda j, m: (0, clip(j, n_up, n_val))
    out_at = lambda j, m: (0, clip(j, n_up + n_val, n_val))
    gate_at = lambda j, m: (0, clip(j, n_up + 2 * n_val, n_val))
    tall = (rows, block)
    shapes = [
        ((rows, hidden), bf16, spec(tall, up_at)),
        ((rows, chans), bf16, spec(tall, val_at)),
        ((rows, chans), bf16, spec(tall, val_at)),
        ((rows, chans), f32, spec(tall, out_at)),
        ((rows, chans), f32, spec(tall, gate_at)),
        ((width // 2, rows), bf16, whole((width // 2, rows))),
        ((width // 2, rows), bf16, whole((width // 2, rows))),
    ]
    if aligned:
        shapes += [((n // 2, size, rows), bf16, whole((n // 2, size, rows)))] * 2
    else:
        shapes += [((hidden, rows), bf16, spec((block, rows), lambda j, m: (clip(j, 0, n_up), 0)))]
    row_no = np.arange(width, dtype=np.int32)[None]
    anywhere = pl.BlockSpec(memory_space=pl.ANY)
    return pl.pallas_call(
        functools.partial(project_kernel, counts, order, aligned),
        grid_spec=pltpu.PrefetchScalarGridSpec(
            num_scalar_prefetch=1,
            grid=(sum(counts),),
            in_specs=[
                whole((rows, width)),
                whole((width,)),
                whole((width,)),
                whole((1, width)),
                whole((1, width)),
                whole((hidden,)),
                whole((chans,)),
                whole((chans,)),
                whole((rows, width)),
                anywhere,
                anywhere,
                anywhere,
                anywhere,
            ],
            out_specs=[s[2] for s in shapes],
            scratch_shapes=[
                pltpu.VMEM((rows, width), bf16),
                pltpu.VMEM((n_up, rows, block), bf16),
                pltpu.VMEM((n_up, width, block), bf16),
                pltpu.VMEM((n_val, width, block), bf16),
                pltpu.VMEM((n_val, block, width), bf16),
                pltpu.VMEM((hidden, chans), bf16),
                pltpu.SemaphoreType.DMA((2 * n_up + 2 * n_val,)),
            ],
        ),
        out_shape=[jax.ShapeDtypeStruct(s[0], s[1]) for s in shapes],
        compiler_params=params(44),
        cost_estimate=took(13),
        name="project",
    )(
        me, tokens, *vectors[:2], jnp.asarray(row_no // (width // n)), jnp.asarray(row_no % (width // n)), *vectors[2:], cot,
        *in_hbm(up_weight, value_weight, out_weight, gate_weight),
    )


def branch_kernel(
    seqs, order, aligned, me, gate_pre, d_gated, val, slope, kern_a, kern_b, skip, ahead, back,
    gated, d_gate, d_val, gate_sum, skip_sum, val_sum, *rest,
):
    *turned, flat, flat_kern = rest
    length = SEQ_LEN
    j = pl.program_id(0)
    block = val.shape[1]
    turn = jnp.where(j < pl.num_programs(0) // 2, 1.0, -1.0).astype(f32)

    def spectrum(a):
        return mm(ahead[...], jnp.concatenate([a, a], axis=0))

    def unspectrum(re, im):
        both = jnp.concatenate([re, im], axis=0)
        high = both.astype(bf16)
        low = (both - high.astype(f32)).astype(bf16)
        two = mm(back[...], high)
        return two[:length] + two[length:] + mm(back[:length], low)

    kern_hat = spectrum(jnp.concatenate([kern_a[0], kern_b[0]], axis=1))
    kr, ki = kern_hat[:length], kern_hat[length:] * turn
    direct = row(skip)
    gr, gi = 0.0, 0.0
    gate_total, skip_total, val_total = 0.0, 0.0, 0.0
    for s in range(seqs):
        rows = slice(s * length, (s + 1) * length)
        v = val[rows]
        v_wide = v.astype(f32)
        hat = spectrum(v)
        vr, vi = hat[:length], hat[length:]
        ssm = unspectrum(kr * vr - ki * vi, kr * vi + ki * vr) + direct * v_wide
        ssm = ssm.astype(bf16).astype(f32)
        g = gate_pre[rows]
        d = d_gated[rows]
        gated_wide = g * ssm
        gated[rows] = gated_wide.astype(bf16)
        flat[pl.ds(j * block, block), rows] = gated_wide.T.astype(bf16)
        dg = (d * ssm).astype(bf16)
        d_gate[rows] = dg
        gate_total = gate_total + jnp.sum(dg.astype(f32), axis=0, keepdims=True)
        ds = (d * g).astype(bf16)
        ds_wide = ds.astype(f32)
        skip_total = skip_total + jnp.sum(ds_wide * v_wide, axis=0, keepdims=True)
        hat = spectrum(ds)
        dr, di = hat[:length], hat[length:]
        back_val = unspectrum(kr * dr + ki * di, kr * di - ki * dr) + direct * ds_wide
        dv = (back_val.astype(bf16).astype(f32) * slope[rows].astype(f32)).astype(bf16)
        d_val[rows] = dv
        val_total = val_total + jnp.sum(dv.astype(f32), axis=0, keepdims=True)
        gr = gr + dr * vr + di * vi
        gi = gi + di * vr - dr * vi
    gate_sum[...] = gate_total
    skip_sum[...] = skip_total
    val_sum[...] = val_total
    flat_kern[pl.ds(j * block, block), :] = unspectrum(gr, gi * turn).T

    @pl.when(j == pl.num_programs(0) - 1)
    def _():
        if aligned:
            own, send, kern_own, kern_send = turned
            scatter_blocks(flat, me[0], order, 0, own, send)
            scatter_blocks(flat_kern, me[0], order, 0, kern_own, kern_send)
        else:
            turned[0][...] = flat[...]
            turned[1][...] = flat_kern[...]


def branch(me, order, skip, gate_pre, d_gated, val, slope, kern):
    rows, chans = val.shape
    n = 1 << len(order)
    seqs = rows // SEQ_LEN
    block = 2 * LANES
    steps = chans // block
    size = chans // n
    aligned = size % 16 == 0
    ahead, back = fourier(SEQ_LEN)
    ahead = jnp.asarray(np.concatenate(in_two(ahead), axis=1))
    back = jnp.asarray(np.concatenate(in_two(back), axis=0))
    tall = spec((rows, block), lambda j, m: (0, j))
    flat = spec((1, block), lambda j, m: (0, j))
    part = chans // 4 // LANES

    def kern_at(k, j, m):
        lane_block = 2 * j + k
        return ((lane_block // part) ^ (m[0] & 3)) * part + lane_block % part, 0, 0

    shapes = [((rows, chans), bf16, tall)] * 3 + [((1, chans), f32, flat)] * 3
    if aligned:
        shapes += [((n // 2, size, rows), bf16, whole((n // 2, size, rows)))] * 2
        shapes += [((n // 2, size, SEQ_LEN), f32, whole((n // 2, size, SEQ_LEN)))] * 2
    else:
        shapes += [((chans, rows), bf16, whole((chans, rows))), ((chans, SEQ_LEN), f32, whole((chans, SEQ_LEN)))]
    return pl.pallas_call(
        functools.partial(branch_kernel, seqs, order, aligned),
        grid_spec=pltpu.PrefetchScalarGridSpec(
            num_scalar_prefetch=1,
            grid=(steps,),
            in_specs=[
                tall,
                tall,
                tall,
                tall,
                spec((1, SEQ_LEN, LANES), functools.partial(kern_at, 0)),
                spec((1, SEQ_LEN, LANES), functools.partial(kern_at, 1)),
                spec((block,), lambda j, m: (j,)),
                whole(ahead.shape),
                whole(back.shape),
            ],
            out_specs=[s[2] for s in shapes],
            scratch_shapes=[pltpu.VMEM((chans, rows), bf16), pltpu.VMEM((chans, SEQ_LEN), f32)],
        ),
        out_shape=[jax.ShapeDtypeStruct(s[0], s[1]) for s in shapes],
        compiler_params=params(16),
        cost_estimate=took(8),
        name="branch",
    )(me, gate_pre, d_gated, val, slope, kern, kern, skip, ahead, back)


def back_kernel(
    d_gate, slope, d_val, tokens, cot, gain, gate_hbm, up_hbm, val_hbm, d_up, up_sum, grad, gain_sum, bias_sum, cot_sum,
    total, gate_w, up_w, val_w, sems,
):
    j = pl.program_id(0)
    steps, block = gate_w.shape[0], gate_w.shape[1]
    copies = []
    for k in range(steps):
        copies.append((gate_hbm.at[pl.ds(k * block, block)], gate_w.at[k]))
        copies.append((up_hbm.at[:, pl.ds(k * block, block)], up_w.at[k]))
    copies.append((val_hbm, val_w))
    copies = [pltpu.make_async_copy(a, b, sems.at[i]) for i, (a, b) in enumerate(copies)]

    @pl.when(j == 0)
    def _():
        for c in copies:
            c.start()

    for k in range(steps):

        @pl.when(j == k)
        def _():
            copies[2 * k].wait()
            copies[2 * k + 1].wait()

    d = (mm_t(d_gate[...], gate_w[j]) * slope[...].astype(f32)).astype(bf16)
    d_up[...] = d
    up_sum[...] = jnp.sum(d.astype(f32), axis=0, keepdims=True)
    more = mm_t(d, up_w[j])

    @pl.when(j == 0)
    def _():
        total[...] = more

    @pl.when(j > 0)
    def _():
        total[...] += more

    @pl.when(j == pl.num_programs(0) - 1)
    def _():
        copies[-1].wait()
        whole_grad = total[...] + mm_t(d_val[...], val_w[...])
        xhat, deviation = norm_of(tokens[...].astype(f32))
        gain_sum[...] = jnp.sum(whole_grad * xhat, axis=0, keepdims=True)
        bias_sum[...] = jnp.sum(whole_grad, axis=0, keepdims=True)
        e = whole_grad * row(gain)
        inner = e - jnp.mean(e, axis=1, keepdims=True) - xhat * jnp.mean(e * xhat, axis=1, keepdims=True)
        wide = cot[...].astype(f32)
        cot_sum[...] = jnp.sum(wide, axis=0, keepdims=True)
        grad[...] = (wide + deviation * inner).astype(bf16)


def back_through(gain, d_gate, slope, d_val, tokens, cot, gate_weight, up_weight, value_weight):
    rows, chans = d_gate.shape
    hidden, width = gate_weight.shape[0], tokens.shape[1]
    block = 512
    steps = hidden // block
    column = lambda j: (0, j)
    flat = whole((1, width))
    anywhere = pl.BlockSpec(memory_space=pl.ANY)
    return pl.pallas_call(
        back_kernel,
        grid=(steps,),
        in_specs=[
            whole((rows, chans)),
            spec((rows, block), column),
            whole((rows, chans)),
            whole((rows, width)),
            whole((rows, width)),
            whole((width,)),
            anywhere,
            anywhere,
            anywhere,
        ],
        out_specs=[spec((rows, block), column), spec((1, block), column), whole((rows, width)), flat, flat, flat],
        out_shape=[
            jax.ShapeDtypeStruct((rows, hidden), bf16),
            jax.ShapeDtypeStruct((1, hidden), f32),
            jax.ShapeDtypeStruct((rows, width), bf16),
        ]
        + [jax.ShapeDtypeStruct((1, width), f32)] * 3,
        scratch_shapes=[
            pltpu.VMEM((rows, width), f32),
            pltpu.VMEM((steps, block, chans), bf16),
            pltpu.VMEM((steps, width, block), bf16),
            pltpu.VMEM((width, chans), bf16),
            pltpu.SemaphoreType.DMA((2 * steps + 1,)),
        ],
        compiler_params=params(32),
        cost_estimate=took(1),
        name="back_through",
    )(d_gate, slope, d_val, tokens, cot, gain, *in_hbm(gate_weight, up_weight, value_weight))


def mixed_kernel(tokens, gated, out_w, bias, mixed):
    mixed[...] = (tokens[...].astype(f32) + mm(gated[...], out_w[...]) + row(bias)).astype(bf16)


def mixed_of(bias, tokens, gated, out_weight):
    rows, width = tokens.shape
    return pl.pallas_call(
        mixed_kernel,
        grid=(1,),
        in_specs=[whole(tokens.shape), whole(gated.shape), whole(out_weight.shape), whole((width,))],
        out_specs=whole(tokens.shape),
        out_shape=jax.ShapeDtypeStruct((rows, width), bf16),
        compiler_params=params(16),
        cost_estimate=took(3),
        name="mixed",
    )(tokens, gated, out_weight, bias)


def kept(shape, dtype=bf16):
    return pltpu.HBM(shape, dtype)


def beside(a, b):
    return jnp.concatenate([a[...], b[...]], axis=1)


def above(a, b):
    return jnp.concatenate([a[...], b[...]], axis=0)


def split_first(g, keep, send):
    half = g.shape[0] // 2
    keep[...] = g[:half]
    send[...] = g[half:]


def split_second(g, keep, send):
    quarter = g.shape[0] // 4
    keep[0] = g[:quarter]
    send[0] = g[quarter : 2 * quarter]
    keep[1] = g[2 * quarter : 3 * quarter]
    send[1] = g[3 * quarter :]


def gate_grad_kernel(lhs_a, lhs_b, rhs_a, rhs_b, keep1, send1, keep2, send2):
    j = pl.program_id(0)
    middle = pl.num_programs(0) // 2
    g = mm(beside(lhs_a, lhs_b), above(rhs_a, rhs_b)).astype(bf16)

    @pl.when(j < middle)
    def _():
        split_first(g, keep1, send1)

    @pl.when(j >= middle)
    def _():
        split_second(g, keep2, send2)


def gate_grad(lhs_a, lhs_b, rhs_a, rhs_b):
    rows, depth = lhs_a.shape
    cols = rhs_a.shape[1]
    block = 384
    steps = cols // block
    middle = steps // 2
    column = spec((depth, block), lambda j: (0, j))
    one = spec((rows // 2, block), lambda j: (0, jnp.minimum(j, middle - 1)))
    two = spec((2, rows // 4, block), lambda j: (0, 0, jnp.maximum(j - middle, 0)))
    return pl.pallas_call(
        gate_grad_kernel,
        grid=(steps,),
        in_specs=[whole((rows, depth))] * 2 + [column] * 2,
        out_specs=[one, one, two, two],
        out_shape=[kept((rows // 2, cols // 2)), jax.ShapeDtypeStruct((rows // 2, cols // 2), bf16)]
        + [kept((2, rows // 4, cols // 2)), jax.ShapeDtypeStruct((2, rows // 4, cols // 2), bf16)],
        compiler_params=params(16),
        cost_estimate=took(6),
        name="gate_grad",
    )(lhs_a, lhs_b, rhs_a, rhs_b)


def input_grad_kernel(n_up, lhs_a, lhs_b, up_a, up_b, val_a, val_b, keep1, send1, keep2, send2):
    j = pl.program_id(0)
    middle = pl.num_programs(0) // 2

    def write(a, b):
        g = mm(beside(lhs_a, lhs_b), above(a, b)).astype(bf16)

        @pl.when(j < middle)
        def _():
            split_first(g, keep1, send1)

        @pl.when(j >= middle)
        def _():
            split_second(g, keep2, send2)

    for use, a, b in ((j < n_up, up_a, up_b), (j >= n_up, val_a, val_b)):

        @pl.when(use)
        def _():
            write(a, b)


def input_grad(lhs_a, lhs_b, up_a, up_b, val_a, val_b, which):
    rows, depth = lhs_a.shape
    hidden, chans = up_a.shape[1], val_a.shape[1]
    cols = (hidden + chans) // 2
    block = 384
    steps, n_up, n_val = cols // block, hidden // block, chans // block
    first, middle = which * steps, steps // 2
    up = spec((depth, block), lambda j: (0, jnp.clip(first + j, 0, n_up - 1)))
    val = spec((depth, block), lambda j: (0, jnp.clip(first + j - n_up, 0, n_val - 1)))
    one = spec((rows // 2, block), lambda j: (0, jnp.minimum(j, middle - 1)))
    two = spec((2, rows // 4, block), lambda j: (0, 0, jnp.maximum(j - middle, 0)))
    return pl.pallas_call(
        functools.partial(input_grad_kernel, n_up - first),
        grid=(steps,),
        in_specs=[whole((rows, depth))] * 2 + [up, up, val, val],
        out_specs=[one, one, two, two],
        out_shape=[kept((rows // 2, cols // 2))] * 2 + [kept((2, rows // 4, cols // 2))] * 2,
        compiler_params=params(16),
        cost_estimate=took(60),
        name="input_grad",
    )(lhs_a, lhs_b, up_a, up_b, val_a, val_b)


def fold_kernel(last, *refs):
    pairs = 2 if len(refs) > 4 else 1
    ins, outs = refs[: 2 * pairs], refs[2 * pairs :]
    at = 0
    for p in range(pairs):
        total = ins[2 * p][...].astype(f32) + ins[2 * p + 1][...].astype(f32)
        columns = slice(at, at + total.shape[1])
        at += total.shape[1]
        if last:
            outs[0][:, columns] = total
        else:
            half = total.shape[0] // 2
            outs[0][:, columns] = total[:half]
            outs[1][:, columns] = total[half:].astype(bf16)


def fold(pairs, last=False, us=0.01):
    rows = pairs[0][0].shape[0]
    cols = sum(p[0].shape[1] for p in pairs)
    if rows % 32:
        total = jnp.concatenate([a.astype(f32) + b.astype(f32) for a, b in pairs], axis=1)
        return total if last else (total[: rows // 2], total[rows // 2 :].astype(bf16))
    if last:
        shapes = jax.ShapeDtypeStruct((rows, cols), f32)
    else:
        shapes = [jax.ShapeDtypeStruct((rows // 2, cols), f32), jax.ShapeDtypeStruct((rows // 2, cols), bf16)]
    return pl.pallas_call(
        functools.partial(fold_kernel, last),
        out_shape=shapes,
        compiler_params=params(16),
        cost_estimate=took(us),
        name="fold",
    )(*[a for p in pairs for a in p])


def pack_kernel(*refs):
    *vectors, out = refs
    at = 0
    for v in vectors:
        lines = v.shape[1] // LANES
        for k in range(lines):
            out[at + k : at + k + 1, :] = v[:, k * LANES : (k + 1) * LANES]
        at += lines


def pack(vectors):
    lines = sum(v.shape[1] for v in vectors) // LANES
    return pl.pallas_call(
        pack_kernel,
        out_shape=jax.ShapeDtypeStruct((lines, LANES), f32),
        compiler_params=params(8),
        cost_estimate=took(0.01),
        name="pack",
    )(*vectors)


def put_wide(wide, keep, send, cols):
    high = wide.astype(bf16)
    low = (wide - high.astype(f32)).astype(bf16)
    half, span = wide.shape[0] // 2, wide.shape[1]
    for part, ref in ((slice(0, half), keep), (slice(half, 2 * half), send)):
        ref[:, cols : cols + span] = high[part]
        ref[:, cols + span :] = low[part]


def out_grad_kernel(lhs_a, lhs_b, rhs_a, rhs_b, kern_a, kern_b, keep, send):
    g = mm(beside(lhs_a, lhs_b), above(rhs_a, rhs_b)).astype(bf16)
    half, cols = g.shape[0] // 2, g.shape[1]
    keep[:, :cols] = g[:half]
    send[:, :cols] = g[half:]
    put_wide(kern_a[...] + kern_b[...], keep, send, cols)


def out_grad(lhs_a, lhs_b, rhs_a, rhs_b, kern_a, kern_b):
    rows, depth = lhs_a.shape
    cols = rhs_a.shape[1] + 2 * kern_a.shape[1]
    return pl.pallas_call(
        out_grad_kernel,
        out_shape=[jax.ShapeDtypeStruct((rows // 2, cols), bf16)] * 2,
        compiler_params=params(16),
        cost_estimate=took(1),
        name="out_grad",
    )(lhs_a, lhs_b, rhs_a, rhs_b, kern_a, kern_b)


def out_add_kernel(cols, last, keep, recv, *outs):
    span = SEQ_LEN
    total = keep[:, :cols].astype(f32) + recv[:, :cols].astype(f32)
    wide = (keep[:, cols : cols + span].astype(f32) + keep[:, cols + span :].astype(f32)) + (
        recv[:, cols : cols + span].astype(f32) + recv[:, cols + span :].astype(f32)
    )
    if last:
        outs[0][...] = total
        outs[1][...] = wide
    else:
        half = total.shape[0] // 2
        outs[0][:, :cols] = total[:half].astype(bf16)
        outs[1][:, :cols] = total[half:].astype(bf16)
        put_wide(wide, *outs, cols)


def out_add(keep, recv, last):
    rows, every = keep.shape
    cols = every - 2 * SEQ_LEN
    if last:
        shapes = [jax.ShapeDtypeStruct((rows, cols), f32), jax.ShapeDtypeStruct((rows, SEQ_LEN), f32)]
    else:
        shapes = [jax.ShapeDtypeStruct((rows // 2, every), bf16)] * 2
    return pl.pallas_call(
        functools.partial(out_add_kernel, cols, last),
        out_shape=shapes,
        compiler_params=params(16),
        cost_estimate=took(0.01),
        name="out_add",
    )(keep, recv)


def param_kernel(me, grad, step, decay, freq, real, imag, g_step, g_decay, g_freq, g_real, g_imag, lags):
    own, chans = grad.shape[0], decay.shape[1]
    window = 2 * LANES
    first = me[0] * own
    start = pl.multiple_of(jnp.minimum(first // LANES * LANES, chans - window), LANES)

    def mine(ref):
        return pltpu.roll(ref[:, pl.ds(start, window)], window - (first - start), 1)[:, :own]

    delta = jnp.exp(pltpu.roll(jnp.broadcast_to(row(step, start, window), (8, window)), window - (first - start), 1)[:1, :own])
    rate, frequency, cr, ci = jnp.exp(mine(decay)), mine(freq), mine(real), mine(imag)
    damp = jnp.exp(-rate * delta)
    angle = frequency * delta
    zr, zi = damp * jnp.cos(angle), damp * jnp.sin(angle)
    lags[...] = grad[...].T
    zero = jnp.zeros_like(zr)

    def body(i, carry):
        pr, pi, dr, di = carry
        g = lags[pl.ds(SEQ_LEN - 1 - i, 1), :]
        dr, di = dr * zr - di * zi + pr, dr * zi + di * zr + pi
        pr, pi = pr * zr - pi * zi + g, pr * zi + pi * zr
        return pr, pi, dr, di

    pr, pi, dr, di = lax.fori_loop(0, SEQ_LEN, body, (zero, zero, zero, zero), unroll=4)
    sr, si = dr * zr - di * zi, dr * zi + di * zr
    ur, ui = cr * sr - ci * si, cr * si + ci * sr
    square = delta * delta
    g_real[...] = (delta * pr).T
    g_imag[...] = (-delta * pi).T
    g_freq[...] = (-square * ui).T
    g_decay[...] = (-square * rate * ur).T
    terms = delta * (cr * pr - ci * pi) - square * (rate * ur + frequency * ui)
    g_step[...] = jnp.sum(terms, axis=0, keepdims=True)


def param_grads(me, grad, step, decay_t, freq_t, real_t, imag_t):
    own, states = grad.shape[0], decay_t.shape[0]
    out = jax.ShapeDtypeStruct((own, states), f32)
    shapes = [jax.ShapeDtypeStruct((1, own), f32)] + [out] * 4
    args = (grad, step, decay_t, freq_t, real_t, imag_t)
    g = pl.pallas_call(
        param_kernel,
        grid_spec=pltpu.PrefetchScalarGridSpec(
            num_scalar_prefetch=1,
            grid=(1,),
            in_specs=[whole(a.shape) for a in args],
            out_specs=[whole(s.shape) for s in shapes],
            scratch_shapes=[pltpu.VMEM((SEQ_LEN, own), f32)],
        ),
        out_shape=shapes,
        compiler_params=params(16),
        cost_estimate=took(3.5),
        name="param_grads",
    )(me, *args)
    return g[0][0], *g[1:]


def local(
    n_dp,
    n_dir,
    tokens,
    layernorm_gain,
    layernorm_bias,
    up_weight,
    up_bias,
    value_weight,
    value_bias,
    step_log,
    decay_log,
    frequency,
    coef_real,
    coef_imag,
    skip_gain,
    gate_weight,
    gate_bias,
    out_weight,
    out_bias,
    cotangent,
):
    rows, width = tokens.shape
    chans = value_weight.shape[1]
    hidden = up_weight.shape[1]
    n = n_dp * n_dir
    nbits = int(math.log2(n))
    me = lax.axis_index("dp") * n_dir + lax.axis_index("dir")
    X, C, Y = 0, 1, 2
    rest = list(range(3, nbits))

    def swap(a, b):
        return lax.ppermute(a, AXES, [(j, j ^ (1 << b)) for j in range(n)])

    main_order = [C, X, Y] + rest
    out_order = [C] + rest + [X, Y]
    own_id = me[None]

    def sorted_halves(flat, order):
        every = jnp.arange(n, dtype=jnp.int32)
        blocks = flat.reshape(n, -1, flat.shape[1])[sort_block(every, me, order)]
        both = blocks.reshape(2, -1, flat.shape[1])
        return both[0], both[1]

    def after(value, *earlier):
        return lax.optimization_barrier((value, *earlier))[0]

    turned_params = [p.T for p in (decay_log, frequency, coef_real, coef_imag)]

    kern = kernel_rows(own_id, step_log, *turned_params)
    pair = jnp.concatenate([kern, swap(kern, C)], axis=0)
    across = swap(pair, X)
    part = kern.shape[0]

    cot_in = swap(cotangent, C)
    up_slope, value_act, value_slope, d_gated, gate_pre, norm_own, norm_send, *turned = project(
        own_id, main_order, (layernorm_gain, layernorm_bias, up_bias, value_bias, gate_bias), after(tokens, cot_in), cotangent, up_weight, value_weight, out_weight, gate_weight
    )
    if len(turned) == 2:
        act_own, act_send = [t.reshape(-1, rows) for t in turned]
    else:
        act_own, act_send = sorted_halves(turned[0], main_order)
    norm_in = swap(norm_send, C)
    act_in = swap(act_send, C)

    pair = after(pair, value_act)
    kern = jnp.concatenate([pair[:part], across[:part], pair[part:], across[part:]], axis=0)
    gated, d_gate, d_value, gate_sum, skip_sum, value_sum, *turned = branch(
        own_id, out_order, skip_gain, gate_pre, d_gated, value_act, value_slope, kern
    )
    if len(turned) == 4:
        gated_own, gated_send, kern_own, kern_send = [t.reshape(-1, t.shape[-1]) for t in turned]
    else:
        gated_own, gated_send = sorted_halves(turned[0], out_order)
        kern_own, kern_send = sorted_halves(turned[1], out_order)
    d_gate_in = swap(d_gate, C)
    gated_in = swap(gated_send, C)
    kern_in = swap(kern_send, C)
    d_value_in = swap(d_value, C)
    mixed = mixed_of(out_bias, tokens, gated, out_weight)

    keep1, send1, keep2, send2 = gate_grad(act_own, act_in, after(d_gate, mixed), d_gate_in)
    keep_o, send_o = out_grad(
        after(gated_own, send1, d_value_in, norm_in), gated_in, cotangent, cot_in, kern_own, kern_in
    )
    d_up, up_sum, grad_tokens, gain_sum, bias_sum, cot_sum = back_through(
        layernorm_gain, after(d_gate, send_o), up_slope, d_value, tokens, cotangent, gate_weight, up_weight, value_weight
    )
    d_up_in = swap(d_up, C)
    order = rest + [X, Y]

    last = [d_up]

    def then(value):
        return after(value, last[0])

    def done(*values):
        last[0] = values[0]
        return values if len(values) > 1 else values[0]

    def fold_next(pairs, final=False, us=0.01):
        first = (then(pairs[0][0]), pairs[0][1])
        result = fold([first] + pairs[1:], final, us)
        return done(result) if final else done(*result)

    def add_next(a, b):
        return done(then(a) + b)

    def out_next(keep, recv, final):
        return done(*out_add(then(keep), recv, final))

    def flat_rows(a):
        return a.reshape(-1, a.shape[-1])

    recv1, recv2, recv_o = swap(send1, X), swap(send2, Y), swap(send_o, order[0])
    keep_o, send_o = out_next(keep_o, recv_o, False)
    recv_o = swap(send_o, order[1])
    keep1, send1 = fold_next([(keep1, recv1)])
    recv1 = swap(send1, Y)
    keep2, send2 = fold_next([(flat_rows(keep2), flat_rows(recv2))], us=30)
    recv2 = swap(send2, X)
    keep1a, send1a, keep2a, send2a = done(*input_grad(norm_own, norm_in, then(d_up), d_up_in, d_value, d_value_in, 0))
    recv1a, recv2a = swap(send1a, X), swap(send2a, Y)
    keep1b, send1b, keep2b, send2b = done(*input_grad(norm_own, norm_in, then(d_up), d_up_in, d_value, d_value_in, 1))
    vectors = [gain_sum, bias_sum, cot_sum, up_sum, value_sum, gate_sum, skip_sum]
    packed = done(pack([then(vectors[0])] + vectors[1:]))
    packed_in = swap(packed, C)
    keep_o, send_o = out_next(keep_o, recv_o, False)
    packed = add_next(packed, packed_in)
    keep, send = fold_next([(keep1, recv1), (keep2, recv2)])
    recv = swap(send, rest[0])
    send1b, send2b = after(send1b, send), after(send2b, send)
    recv1b, recv2b = swap(send1b, X), swap(send2b, Y)
    keep1a, send1a = fold_next([(keep1a, recv1a)])
    recv1a = swap(send1a, Y)
    keep2a, send2a = fold_next([(flat_rows(keep2a), flat_rows(recv2a))])
    recv2a = swap(send2a, X)
    keep, send = fold_next([(keep, recv)])
    recv = swap(send, rest[1])
    keep1b, send1b = fold_next([(keep1b, recv1b)])
    recv1b = swap(send1b, Y)
    keep2b, send2b = fold_next([(flat_rows(keep2b), flat_rows(recv2b))])
    recv2b = swap(send2b, X)
    keep_a, send_a = fold_next([(keep1a, recv1a), (keep2a, recv2a)])
    recv_a = swap(send_a, rest[0])
    packed_in = swap(after(packed, send_a), X)
    recv_o = swap(after(send_o, send_a), order[2])
    keep_b, send_b = fold_next([(keep1b, recv1b), (keep2b, recv2b)])
    recv_b = swap(send_b, rest[0])
    packed = add_next(packed, packed_in)
    packed_in = swap(packed, Y)
    for b in rest[2:]:
        keep, send = fold_next([(keep, recv)])
        recv = swap(send, b)
    gate_share = fold_next([(keep, recv)], True)
    keep_a, send_a = fold_next([(keep_a, recv_a)])
    recv_a = swap(send_a, rest[1])
    for b in order[3:]:
        keep_o, send_o = out_next(keep_o, recv_o, False)
        recv_o = swap(send_o, b)
    packed = add_next(packed, packed_in)
    packed_in = swap(packed, rest[0])
    packed = add_next(packed, packed_in)
    packed_in = swap(packed, rest[1])
    keep_b, send_b = fold_next([(keep_b, recv_b)])
    recv_b = swap(after(send_b, packed), rest[1])
    for b in rest[2:]:
        keep_a, send_a = fold_next([(keep_a, recv_a)])
        recv_a = swap(send_a, b)
    out_share, grad_kern = out_next(keep_o, recv_o, True)
    share_a = fold_next([(keep_a, recv_a)], True)
    packed = add_next(packed, packed_in)
    for b in rest[2:]:
        packed = add_next(packed, swap(packed, b))
        keep_b, send_b = fold_next([(keep_b, recv_b)])
        recv_b = swap(send_b, b)
    share_b = fold_next([(keep_b, recv_b)], True)
    input_share = jnp.concatenate([share_a, share_b], axis=1)

    packed = packed.reshape(-1)
    sums, at = [], 0
    for v in vectors:
        sums.append(packed[at : at + v.shape[1]])
        at += v.shape[1]

    def share(v):
        size = v.shape[0] // n
        return lax.dynamic_slice_in_dim(v, me * size, size, 0)

    steps, decays, frequencies, reals, imags = param_grads(own_id, grad_kern, step_log, *turned_params)
    return (
        mixed,
        grad_tokens,
        sums[0],
        sums[1],
        input_share[:, :hidden],
        share(sums[3]),
        input_share[:, hidden:],
        share(sums[4]),
        steps,
        decays,
        frequencies,
        reals,
        imags,
        share(sums[6]),
        gate_share,
        share(sums[5]),
        out_share,
        sums[2],
    )


def solution(mesh):
    n_dp, n_dir = mesh.shape["dp"], mesh.shape["dir"]
    split, replicated = P(AXES), P()
    in_specs = (split,) + (replicated,) * 16 + (split,)
    out_specs = (split, split, replicated, replicated) + (split,) * 13 + (replicated,)

    def run(*args):
        return local(n_dp, n_dir, *args)

    return jax.shard_map(run, mesh=mesh, in_specs=in_specs, out_specs=out_specs, check_vma=False)
```
